32 devices in a mesh: grp: 16 (over z, x, core), rep: 2 (over y).
Axes of the slice: x: 2, y: 2, z: 4, core: 2. Of those that a mesh axis runs over, the one named last changes fastest.
Arguments:
- adjoint: bfloat16 [256, 512], P('grp'), may hold values from -6 to 6
- active: int32 [256, 512], P('grp'), may hold values 0 or 1
- counts: int32 [256, 16384], P('rep', 'grp'), may hold values from 0 to 3, as said below
- src_degree: int32 [256], P('rep'), may hold values from 8 to 256
- dst_degree: int32 [16384], P('grp'), may hold values from 8 to 256
- inputs: bfloat16 [16384, 512], P(('grp', 'rep')), may hold values from -6 to 6
- weight: bfloat16 [512, 512], replicated, may hold values from -0.25 to 0.25
Outputs:
- grad_input: bfloat16 [16384, 512], P(('grp', 'rep'))
- grad_weight: float32 [512, 512], P('rep')
The draws below stay inside these ranges and needn't reach their ends.
Inputs may be any that keep to these rules, and one draw needn't show every extreme that they name: Edge counts; within an aligned tile of 16 source rows by 1024 destination columns the share of nonzero entries ranges from none to all, differing from tile to tile.
All inputs are finite; a program needn't handle non-finite values. No bound on the sum of `active` on one device may be relied on, other than what follows from the above.
Results may differ from the reference program's by a relative error of at most 0.0057.
Values may be sent and summed in bfloat16 or wider, within the bound.
No kernel may reach another device: no remote copies, remote signals or barrier semaphores. Data moves between devices by JAX's collectives and lax.ppermute only.
A program may use at most 64 MiB of HBM per device.

```python
import jax
import jax.numpy as jnp
from jax import lax

F = 512
VS = 16
VD = 1024
NSRC = 256
NDST = 16384


def draw_counts(key, part):
    level_key, entry_key = jax.random.split(jax.random.fold_in(key, 11))
    src_blocks = NSRC // VS
    dst_blocks = NDST // VD
    levels = jax.random.randint(level_key, (src_blocks, 1, dst_blocks, 1), 0, 9)
    entries = jax.random.randint(entry_key, (src_blocks, VS, dst_blocks, VD), 0, 24)
    edges = jnp.where(entries % 8 < levels, entries // 8 + 1, 0)
    return edges.reshape(NSRC, NDST).astype(jnp.int32)


def touch_ends(result, stream_key, least, top_value):
    spot = [jax.random.randint(jax.random.fold_in(stream_key, axis), (), 0, length) for axis, length in enumerate(result.shape)]
    longest = result.shape.index(max(result.shape))
    beside = spot[:longest] + [(spot[longest] + 1) % result.shape[longest]] + spot[longest + 1:]
    return result.at[tuple(spot)].set(least).at[tuple(beside)].set(top_value)


def level_of(key, shape, shards, low, top_value):
    loudness, own = 1.0, jax.random.fold_in(key, 6)
    for axis_at, parts in shards:
        steps = jnp.exp(jax.random.uniform(jax.random.fold_in(own, axis_at), (parts,), jnp.float32, low / len(shards), top_value / len(shards)))
        loudness = loudness * jnp.repeat(steps, shape[axis_at] // parts).reshape([-1 if axis == axis_at else 1 for axis in range(len(shape))])
    return loudness


def scatter_about(own_key, extent, scale, most, cuts=(), kind=jnp.bfloat16):
    values = jax.random.normal(own_key, extent, jnp.float32) * scale
    if len(cuts) > 0:
        values = level_of(own_key, extent, cuts, -0.22, 0.18) * values
    return jnp.clip(values, min=-most, max=most).astype(kind)


def setup_inputs(seed: int = 0) -> dict:
    key_list = jax.random.split(jax.random.key(seed), 8)
    return {
        "adjoint": scatter_about(key_list[0], (NSRC, F), 1.0, 6.0, ((0, 16),)),
        "active": touch_ends((jax.random.randint(key_list[1], (NSRC, F), 0, 2) < 1).astype(jnp.int32), jax.random.fold_in(key_list[1], 1), 0, 1),
        "counts": draw_counts(jax.random.fold_in(key_list[7], 71), 0),
        "src_degree": touch_ends(jax.random.randint(key_list[3], (NSRC,), 8, 257), jax.random.fold_in(key_list[3], 1), 8, 256).astype(jnp.int32),
        "dst_degree": touch_ends(jax.random.randint(key_list[4], (NDST,), 8, 257), jax.random.fold_in(key_list[4], 1), 8, 256).astype(jnp.int32),
        "inputs": scatter_about(key_list[5], (NDST, F), 1.0, 6.0, ((0, 32),)),
        "weight": scatter_about(key_list[6], (F, F), F ** -0.5, 0.25),
    }


def reference(adjoint, active, counts, src_degree, dst_degree, inputs, weight):
    masked = (adjoint.astype(jnp.float32) * active.astype(jnp.float32)).astype(jnp.bfloat16)
    src_scale = lax.rsqrt(src_degree.astype(jnp.float32))
    dst_scale = lax.rsqrt(dst_degree.astype(jnp.float32))
    vertex_total = inputs.shape[0]
    dst_blocks = vertex_total // VD

    def one_block(block_index):
        start = (block_index * VD).astype(jnp.int32)
        count_tile = lax.dynamic_slice_in_dim(counts, start, VD, 1).astype(jnp.float32)
        col_scale = lax.dynamic_slice_in_dim(dst_scale, start, VD, 0)
        scaled_tile = (count_tile * src_scale[:, None] * col_scale[None, :]).astype(jnp.bfloat16)
        return lax.dot_general(scaled_tile, masked, (((0,), (0,)), ((), ())), preferred_element_type=jnp.float32)
    grad_pre = lax.map(one_block, jnp.arange(dst_blocks, dtype=jnp.int32)).reshape(vertex_total, F)
    grad_high = grad_pre.astype(jnp.bfloat16)
    grad_low = (grad_pre - grad_high.astype(jnp.float32)).astype(jnp.bfloat16)
    grad_input = lax.dot_general(grad_high, weight, (((1,), (1,)), ((), ())), preferred_element_type=jnp.float32).astype(jnp.bfloat16)
    upper = lax.dot_general(inputs, grad_high, (((0,), (0,)), ((), ())), preferred_element_type=jnp.float32)
    lower = lax.dot_general(inputs, grad_low, (((0,), (0,)), ((), ())), preferred_element_type=jnp.float32)
    grad_weight = (upper + lower) / vertex_total
    return (grad_input, grad_weight)
```

```python
import jax
import jax.numpy as jnp
from jax import lax
from jax.sharding import PartitionSpec as P


def swap(block, axis, step):
    size = lax.axis_size(axis)
    return lax.ppermute(block, axis, [(at, at ^ step) for at in range(size)])


def bit_of(index, step):
    return (index & step) != 0


def in_order(upper, mine, theirs, axis):
    return jnp.where(
        upper,
        jnp.concatenate([theirs, mine], axis),
        jnp.concatenate([mine, theirs], axis),
    )


def half_of(block, axis, upper):
    size = block.shape[axis] // 2
    low = lax.slice_in_dim(block, 0, size, axis=axis)
    high = lax.slice_in_dim(block, size, 2 * size, axis=axis)
    return jnp.where(upper, high, low)


def matmul(left, right, contract):
    return lax.dot_general(
        left, right, (contract, ((), ())), preferred_element_type=jnp.float32
    )


def body(adjoint, active, counts, src_degree, dst_degree, inputs, weight):
    groups, replicas = lax.axis_size("grp"), lax.axis_size("rep")
    group, replica = lax.axis_index("grp"), lax.axis_index("rep")
    width = inputs.shape[1]
    rows = inputs.shape[0]
    block_rows = adjoint.shape[0]

    src_scale = lax.rsqrt(src_degree.astype(jnp.float32))
    dst_scale = lax.rsqrt(dst_degree.astype(jnp.float32))

    def scaled_part(owner):
        part = lax.dynamic_slice_in_dim(counts, owner * rows, rows, 1)
        col = lax.dynamic_slice_in_dim(dst_scale, owner * rows, rows, 0)
        return (part.astype(jnp.float32) * src_scale[:, None] * col[None, :]).astype(jnp.bfloat16)

    parts = [scaled_part(replica)]
    for step in range(1, replicas):
        parts.append(swap(scaled_part(replica ^ step), "rep", step))
    masked = (adjoint.astype(jnp.float32) * active.astype(jnp.float32)).astype(jnp.bfloat16)

    terms = [matmul(part, inputs, ((1,), (0,))) for part in parts]

    def ordered(pieces):
        step = 1
        while len(pieces) > 1:
            upper = bit_of(replica, step)
            pieces = [in_order(upper, a, b, 0) for a, b in zip(pieces[0::2], pieces[1::2])]
            step *= 2
        return pieces[0]

    scaled = ordered(parts)
    total = ordered(terms)

    odd = bit_of(group, 1)
    pairs = total.reshape(groups // 2, 2, block_rows, width)
    even_half = pairs[:, 0].reshape(-1, width)
    odd_half = pairs[:, 1].reshape(-1, width)
    theirs = swap(jnp.where(odd, even_half, odd_half).astype(jnp.bfloat16), "grp", 1)
    total = jnp.where(odd, odd_half, even_half) + theirs.astype(jnp.float32)

    step = replicas // 2
    while step:
        upper = bit_of(replica, step)
        theirs = swap(half_of(total, 1, ~upper).astype(jnp.bfloat16), "rep", step)
        total = half_of(total, 1, upper) + theirs.astype(jnp.float32)
        step //= 2

    step = groups // 2
    gathered = masked
    kept = total.shape
    while step > 1:
        sent = total.astype(jnp.bfloat16)
        flat = sent.reshape(-1, width) if kept[1] == width else jnp.concatenate(
            jnp.split(sent, width // kept[1], axis=0), axis=1
        )
        answer = swap(jnp.concatenate([flat, gathered], axis=0), "grp", step)
        back = answer[: flat.shape[0]]
        back = jnp.concatenate(jnp.split(back, width // kept[1], axis=1), axis=0)
        total = sent.astype(jnp.float32) + back.astype(jnp.float32)
        gathered = (gathered, answer[flat.shape[0]:])
        upper = bit_of(group, step)
        mine = gathered[0].reshape(-1, 1, block_rows, width)
        other = gathered[1].reshape(-1, 1, block_rows, width)
        gathered = in_order(upper, mine, other, 1).reshape(-1, width)
        step //= 2

    both = jnp.concatenate([total.astype(jnp.bfloat16), gathered], axis=1)
    other = swap(both, "grp", 1)
    cols = both.shape[1]
    both = in_order(
        odd, both.reshape(-1, 1, block_rows, cols), other.reshape(-1, 1, block_rows, cols), 1
    ).reshape(-1, cols)
    total, gathered = both[:, : kept[1]], both[:, kept[1]:]

    grad_pre = matmul(scaled, gathered, ((0,), (0,)))
    grad_input = matmul(grad_pre.astype(jnp.bfloat16), weight, ((1,), (1,))).astype(jnp.bfloat16)
    vertex_total = rows * groups * replicas
    grad_weight = matmul(total, gathered, ((0,), (0,))) / vertex_total
    return (grad_input, grad_weight)


def solution(mesh):
    in_specs = (
        P("grp", None),
        P("grp", None),
        P("rep", "grp"),
        P("rep"),
        P("grp"),
        P(("grp", "rep"), None),
        P(),
    )
    out_specs = (P(("grp", "rep"), None), P("rep", None))
    return jax.shard_map(body, mesh=mesh, in_specs=in_specs, out_specs=out_specs, check_vma=False)
```

```python
import functools

import jax
import jax.numpy as jnp
from jax import lax
from jax.experimental import pallas as pl
from jax.experimental.pallas import tpu as pltpu
from jax.sharding import PartitionSpec as P


def swap(block, axis, step):
    size = lax.axis_size(axis)
    return lax.ppermute(block, axis, [(at, at ^ step) for at in range(size)])


def bit_of(index, step):
    return (index & step) != 0


def in_order(upper, mine, theirs, axis):
    return jnp.where(
        upper,
        jnp.concatenate([theirs, mine], axis),
        jnp.concatenate([mine, theirs], axis),
    )


def half_of(block, axis, upper):
    size = block.shape[axis] // 2
    low = lax.slice_in_dim(block, 0, size, axis=axis)
    high = lax.slice_in_dim(block, size, 2 * size, axis=axis)
    return jnp.where(upper, high, low)


def part_of(block, axis, index, parts):
    step = parts // 2
    while step:
        block = half_of(block, axis, bit_of(index, step))
        step //= 2
    return block


def matmul(left, right, contract):
    return lax.dot_general(
        left, right, (contract, ((), ())), preferred_element_type=jnp.float32
    )


CHUNKS = 4


def prepare_kernel(replicas, counts, src_degree, dst_degree, *refs):
    outs, (count_part, src_part, dst_part, sems) = refs[:replicas], refs[replicas:]
    src_rows, rows = outs[0].shape
    piece = src_rows // CHUNKS
    replica = lax.axis_index("rep")
    owners = [replica ^ step for step in range(1, replicas)] + [replica]
    degrees = [
        pltpu.make_async_copy(src_degree, src_part, sems.at[0]),
        pltpu.make_async_copy(dst_degree, dst_part, sems.at[1]),
    ]
    for copy in degrees:
        copy.start()
    copies = []
    for slot, owner in enumerate(owners):
        columns = pl.ds(pl.multiple_of(owner * rows, 128), rows)
        for chunk in range(CHUNKS):
            at = pl.ds(chunk * piece, piece)
            copy = pltpu.make_async_copy(
                counts.at[at, columns], count_part.at[slot, at], sems.at[2 + slot * CHUNKS + chunk]
            )
            copy.start()
            copies.append(copy)
    for copy in degrees:
        copy.wait()
    src_row = lax.rsqrt(src_part[...].astype(jnp.float32)).reshape(1, src_rows)
    square = (src_rows, src_rows)
    diagonal = lax.broadcasted_iota(jnp.int32, square, 0) == lax.broadcasted_iota(jnp.int32, square, 1)
    src_column = jnp.sum(
        jnp.where(diagonal, jnp.broadcast_to(src_row, square), 0.0), axis=1, keepdims=True
    )
    for slot, owner in enumerate(owners):
        pieces = [dst_part[at * rows : (at + 1) * rows] for at in range(replicas)]
        bit = 1
        while len(pieces) > 1:
            upper = bit_of(owner, bit)
            pieces = [jnp.where(upper, b, a) for a, b in zip(pieces[0::2], pieces[1::2])]
            bit *= 2
        dst_row = lax.rsqrt(pieces[0].astype(jnp.float32)).reshape(1, rows)
        for chunk in range(CHUNKS):
            at = slice(chunk * piece, (chunk + 1) * piece)
            copies[slot * CHUNKS + chunk].wait()
            values = count_part[slot, at, :].astype(jnp.float32)
            outs[slot][at, :] = (values * src_column[at] * dst_row).astype(jnp.bfloat16)


def prepare(counts, src_degree, dst_degree, replicas, rows):
    src_rows = counts.shape[0]
    return pl.pallas_call(
        functools.partial(prepare_kernel, replicas),
        out_shape=[pltpu.VMEM((src_rows, rows), jnp.bfloat16)] * replicas,
        in_specs=[pl.BlockSpec(memory_space=pl.ANY)] * 3,
        out_specs=[pl.BlockSpec(memory_space=pltpu.VMEM)] * replicas,
        scratch_shapes=[
            pltpu.VMEM((replicas, src_rows, rows), jnp.int32),
            pltpu.VMEM(src_degree.shape, jnp.int32),
            pltpu.VMEM(dst_degree.shape, jnp.int32),
            pltpu.SemaphoreType.DMA((2 + CHUNKS * replicas,)),
        ],
    )(counts, src_degree, dst_degree)


def own_kernel(own, inputs, term):
    term[...] = jnp.dot(own[...], inputs[...], preferred_element_type=jnp.float32)


def own_product(own, inputs):
    (src_rows, rows), width = own.shape, inputs.shape[1]
    return pl.pallas_call(
        own_kernel,
        out_shape=pltpu.VMEM((src_rows, width), jnp.float32),
        in_specs=[pl.BlockSpec(memory_space=pltpu.VMEM)] * 2,
        out_specs=pl.BlockSpec(memory_space=pltpu.VMEM),
        cost_estimate=pl.CostEstimate(
            flops=2 * src_rows * rows * width,
            bytes_accessed=2 * rows * (src_rows + width),
            transcendentals=0,
        ),
    )(*[pltpu.with_memory_space_constraint(block, pltpu.VMEM) for block in (own, inputs)])


def body(adjoint, active, counts, src_degree, dst_degree, inputs, weight):
    groups, replicas = lax.axis_size("grp"), lax.axis_size("rep")
    group, replica = lax.axis_index("grp"), lax.axis_index("rep")
    rows, width = inputs.shape
    block_rows = adjoint.shape[0]
    odd = bit_of(group, 1)

    *sent, own = prepare(counts, src_degree, dst_degree, replicas, rows)
    answers = [swap(part, "rep", step) for step, part in enumerate(sent, 1)]

    own_term = own_product(own, inputs)
    masked = (adjoint.astype(jnp.float32) * active.astype(jnp.float32)).astype(jnp.bfloat16)

    def gathered(mine, theirs, step):
        return in_order(
            bit_of(group, step),
            mine.reshape(-1, 1, block_rows, width),
            theirs.reshape(-1, 1, block_rows, width),
            1,
        ).reshape(-1, width)

    far = groups // 2
    theirs = swap(masked, "grp", far) if far > 1 else masked
    answers, own_term = lax.optimization_barrier((answers, own_term))
    parts = [own] + answers
    terms = [own_term] + [matmul(part, inputs, ((1,), (0,))) for part in answers]

    def ordered(pieces):
        step = 1
        while len(pieces) > 1:
            upper = bit_of(replica, step)
            pieces = [in_order(upper, a, b, 0) for a, b in zip(pieces[0::2], pieces[1::2])]
            step *= 2
        return pieces[0]

    def halves(block):
        pairs = block.reshape(groups // 2, 2, block_rows, block.shape[1])
        even = pairs[:, 0].reshape(-1, block.shape[1])
        uneven = pairs[:, 1].reshape(-1, block.shape[1])
        return jnp.where(odd, uneven, even), jnp.where(odd, even, uneven)

    kept, sent = halves(ordered(terms))
    total = kept + swap(sent.astype(jnp.bfloat16), "grp", 1).astype(jnp.float32)

    total, theirs = lax.optimization_barrier((total, theirs))
    mine = gathered(masked, theirs, far) if far > 1 else masked

    step = replicas // 2
    while step:
        upper = bit_of(replica, step)
        theirs = swap(half_of(total, 1, ~upper).astype(jnp.bfloat16), "rep", step)
        total = half_of(total, 1, upper) + theirs.astype(jnp.float32)
        step //= 2

    step = far // 2
    while step > 1:
        sent = total.astype(jnp.bfloat16)
        flat = jnp.concatenate(jnp.split(sent, replicas, axis=0), axis=1)
        answer = swap(jnp.concatenate([flat, mine], axis=0), "grp", step)
        count = flat.shape[0]
        theirs = jnp.concatenate(jnp.split(answer[:count], replicas, axis=1), axis=0)
        total = sent.astype(jnp.float32) + theirs.astype(jnp.float32)
        mine = gathered(mine, answer[count:], step)
        step //= 2
    theirs = swap(mine, "grp", 1)
    scaled_mine, scaled_theirs = halves(ordered(parts))
    grad_pre = matmul(scaled_mine, mine, ((0,), (0,)))
    grad_pre += matmul(scaled_theirs, theirs, ((0,), (0,)))
    grad_input = matmul(grad_pre.astype(jnp.bfloat16), weight, ((1,), (1,))).astype(jnp.bfloat16)
    if far > 1:
        sent = total.astype(jnp.bfloat16)
        answer = swap(sent, "grp", far)
        answer, grad_input = lax.optimization_barrier((answer, grad_input))
        total = sent.astype(jnp.float32) + answer.astype(jnp.float32)

    total = total.astype(jnp.bfloat16)
    other = swap(total, "grp", 1)
    vertex_total = rows * groups * replicas
    grad_weight = matmul(total, mine, ((0,), (0,))) + matmul(other, theirs, ((0,), (0,)))
    return (grad_input, grad_weight / vertex_total)


def solution(mesh):
    in_specs = (
        P("grp", None),
        P("grp", None),
        P("rep", "grp"),
        P("rep"),
        P("grp"),
        P(("grp", "rep"), None),
        P(),
    )
    out_specs = (P(("grp", "rep"), None), P("rep", None))
    return jax.shard_map(body, mesh=mesh, in_specs=in_specs, out_specs=out_specs, check_vma=False)
```

```python
import functools

import jax
import jax.numpy as jnp
from jax import lax
from jax.experimental import pallas as pl
from jax.experimental.pallas import tpu as pltpu
from jax.sharding import PartitionSpec as P


def swap(block, axis, step):
    size = lax.axis_size(axis)
    return lax.ppermute(block, axis, [(at, at ^ step) for at in range(size)])


def bit_of(index, step):
    return (index & step) != 0


def in_order(upper, mine, theirs, axis):
    return jnp.where(
        upper,
        jnp.concatenate([theirs, mine], axis),
        jnp.concatenate([mine, theirs], axis),
    )


def half_of(block, axis, upper):
    size = block.shape[axis] // 2
    low = lax.slice_in_dim(block, 0, size, axis=axis)
    high = lax.slice_in_dim(block, size, 2 * size, axis=axis)
    return jnp.where(upper, high, low)


def part_of(block, axis, index, parts):
    step = parts // 2
    while step:
        block = half_of(block, axis, bit_of(index, step))
        step //= 2
    return block


def matmul(left, right, contract):
    return lax.dot_general(
        left, right, (contract, ((), ())), preferred_element_type=jnp.float32
    )


CHUNKS = 4


def prepare_kernel(replicas, counts, src_degree, dst_degree, *refs):
    outs, (count_part, src_part, dst_part, sems) = refs[:replicas], refs[replicas:]
    src_rows, rows = outs[0].shape
    piece = src_rows // CHUNKS
    replica = lax.axis_index("rep")
    owners = [replica ^ step for step in range(1, replicas)] + [replica]
    degrees = [
        pltpu.make_async_copy(src_degree, src_part, sems.at[0]),
        pltpu.make_async_copy(dst_degree, dst_part, sems.at[1]),
    ]
    for copy in degrees:
        copy.start()
    copies = []
    for slot, owner in enumerate(owners):
        columns = pl.ds(pl.multiple_of(owner * rows, 128), rows)
        for chunk in range(CHUNKS):
            at = pl.ds(chunk * piece, piece)
            copy = pltpu.make_async_copy(
                counts.at[at, columns], count_part.at[slot, at], sems.at[2 + slot * CHUNKS + chunk]
            )
            copy.start()
            copies.append(copy)
    for copy in degrees:
        copy.wait()
    src_row = lax.rsqrt(src_part[...].astype(jnp.float32)).reshape(1, src_rows)
    square = (src_rows, src_rows)
    diagonal = lax.broadcasted_iota(jnp.int32, square, 0) == lax.broadcasted_iota(jnp.int32, square, 1)
    src_column = jnp.sum(
        jnp.where(diagonal, jnp.broadcast_to(src_row, square), 0.0), axis=1, keepdims=True
    )
    for slot, owner in enumerate(owners):
        pieces = [dst_part[at * rows : (at + 1) * rows] for at in range(replicas)]
        bit = 1
        while len(pieces) > 1:
            upper = bit_of(owner, bit)
            pieces = [jnp.where(upper, b, a) for a, b in zip(pieces[0::2], pieces[1::2])]
            bit *= 2
        dst_row = lax.rsqrt(pieces[0].astype(jnp.float32)).reshape(1, rows)
        for chunk in range(CHUNKS):
            at = slice(chunk * piece, (chunk + 1) * piece)
            copies[slot * CHUNKS + chunk].wait()
            values = count_part[slot, at, :].astype(jnp.float32)
            outs[slot][at, :] = (values * src_column[at] * dst_row).astype(jnp.bfloat16)


def prepare(counts, src_degree, dst_degree, replicas, rows):
    src_rows = counts.shape[0]
    return pl.pallas_call(
        functools.partial(prepare_kernel, replicas),
        out_shape=[pltpu.VMEM((src_rows, rows), jnp.bfloat16)] * replicas,
        in_specs=[pl.BlockSpec(memory_space=pl.ANY)] * 3,
        out_specs=[pl.BlockSpec(memory_space=pltpu.VMEM)] * replicas,
        scratch_shapes=[
            pltpu.VMEM((replicas, src_rows, rows), jnp.int32),
            pltpu.VMEM(src_degree.shape, jnp.int32),
            pltpu.VMEM(dst_degree.shape, jnp.int32),
            pltpu.SemaphoreType.DMA((2 + CHUNKS * replicas,)),
        ],
    )(counts, src_degree, dst_degree)


def own_kernel(own, inputs, term):
    term[...] = jnp.dot(own[...], inputs[...], preferred_element_type=jnp.float32)


def own_product(own, inputs):
    (src_rows, rows), width = own.shape, inputs.shape[1]
    return pl.pallas_call(
        own_kernel,
        out_shape=pltpu.VMEM((src_rows, width), jnp.float32),
        in_specs=[pl.BlockSpec(memory_space=pltpu.VMEM)] * 2,
        out_specs=pl.BlockSpec(memory_space=pltpu.VMEM),
        cost_estimate=pl.CostEstimate(
            flops=2 * src_rows * rows * width,
            bytes_accessed=2 * rows * (src_rows + width),
            transcendentals=0,
        ),
    )(*[pltpu.with_memory_space_constraint(block, pltpu.VMEM) for block in (own, inputs)])


def body(adjoint, active, counts, src_degree, dst_degree, inputs, weight):
    groups, replicas = lax.axis_size("grp"), lax.axis_size("rep")
    group, replica = lax.axis_index("grp"), lax.axis_index("rep")
    rows, width = inputs.shape
    block_rows = adjoint.shape[0]
    odd = bit_of(group, 1)

    *sent, own = prepare(counts, src_degree, dst_degree, replicas, rows)
    answers = [swap(part, "rep", step) for step, part in enumerate(sent, 1)]

    own_term = own_product(own, inputs)
    masked = (adjoint.astype(jnp.float32) * active.astype(jnp.float32)).astype(jnp.bfloat16)

    def gathered(mine, theirs, step):
        run = block_rows * (2 if 2 < step < groups // 2 else 1)
        return in_order(
            bit_of(group, step),
            mine.reshape(-1, 1, run, width),
            theirs.reshape(-1, 1, run, width),
            1,
        ).reshape(-1, width)

    far = groups // 2
    theirs = swap(masked, "grp", far) if far > 1 else masked
    answers, own_term = lax.optimization_barrier((answers, own_term))
    parts = [own] + answers
    terms = [own_term] + [matmul(part, inputs, ((1,), (0,))) for part in answers]

    def ordered(pieces):
        step = 1
        while len(pieces) > 1:
            upper = bit_of(replica, step)
            pieces = [in_order(upper, a, b, 0) for a, b in zip(pieces[0::2], pieces[1::2])]
            step *= 2
        return pieces[0]

    def halves(block):
        pairs = block.reshape(groups // 2, 2, block_rows, block.shape[1])
        even = pairs[:, 0].reshape(-1, block.shape[1])
        uneven = pairs[:, 1].reshape(-1, block.shape[1])
        return jnp.where(odd, uneven, even), jnp.where(odd, even, uneven)

    kept, sent = halves(ordered(terms))
    total = kept + swap(sent.astype(jnp.bfloat16), "grp", 1).astype(jnp.float32)

    total, theirs = lax.optimization_barrier((total, theirs))
    mine = gathered(masked, theirs, far) if far > 1 else masked

    near = None
    step = replicas // 2
    while step:
        upper = bit_of(replica, step)
        sent = half_of(total, 1, ~upper).astype(jnp.bfloat16)
        if step == 1 and far > 2:
            sent, mine = lax.optimization_barrier((sent, mine))
            near, near_step = swap(mine, "grp", 2), 2
        theirs = swap(sent, "rep", step)
        total = half_of(total, 1, upper) + theirs.astype(jnp.float32)
        step //= 2

    steps = [far >> at for at in range(1, far.bit_length() - 1)] + [far] * (far > 1)
    for step in steps:
        sent = total.astype(jnp.bfloat16)
        answer = swap(sent, "grp", step)
        if near is not None:
            sent, near = lax.optimization_barrier((sent, near))
            mine, near = gathered(mine, near, near_step), None
        if 2 * step < far:
            near, near_step = swap(mine, "grp", 2 * step), 2 * step
        if step == far:
            theirs = swap(mine, "grp", 1)
            scaled_mine, scaled_theirs = halves(ordered(parts))
            grad_pre = matmul(scaled_mine, mine, ((0,), (0,)))
            grad_pre += matmul(scaled_theirs, theirs, ((0,), (0,)))
            grad_input = matmul(grad_pre.astype(jnp.bfloat16), weight, ((1,), (1,)))
            answer, grad_input = lax.optimization_barrier((answer, grad_input.astype(jnp.bfloat16)))
        total = sent.astype(jnp.float32) + answer.astype(jnp.float32)

    total = total.astype(jnp.bfloat16)
    other = swap(total, "grp", 1)
    vertex_total = rows * groups * replicas
    grad_weight = matmul(total, mine, ((0,), (0,))) + matmul(other, theirs, ((0,), (0,)))
    return (grad_input, grad_weight / vertex_total)


def solution(mesh):
    in_specs = (
        P("grp", None),
        P("grp", None),
        P("rep", "grp"),
        P("rep"),
        P("grp"),
        P(("grp", "rep"), None),
        P(),
    )
    out_specs = (P(("grp", "rep"), None), P("rep", None))
    return jax.shard_map(body, mesh=mesh, in_specs=in_specs, out_specs=out_specs, check_vma=False)
```

```python
import functools

import jax
import jax.numpy as jnp
from jax import lax
from jax.experimental import pallas as pl
from jax.experimental.pallas import tpu as pltpu
from jax.sharding import PartitionSpec as P


def swap(block, axis, step):
    size = lax.axis_size(axis)
    return lax.ppermute(block, axis, [(at, at ^ step) for at in range(size)])


def parity(number):
    count = 0
    while number:
        count ^= number & 1
        number >>= 1
    return count


def crossed(block, group_steps, replica_step):
    groups, replicas = lax.axis_size("grp"), lax.axis_size("rep")
    pairs = []
    for group in range(groups):
        for replica in range(replicas):
            step = group_steps[parity(group) ^ parity(replica)] | 1
            pairs.append((group * replicas + replica, (group ^ step) * replicas + (replica ^ replica_step)))
    return lax.ppermute(block, ("grp", "rep"), pairs)


def bit_of(index, step):
    return (index & step) != 0


def in_order(upper, mine, theirs, axis):
    return jnp.where(
        upper,
        jnp.concatenate([theirs, mine], axis),
        jnp.concatenate([mine, theirs], axis),
    )


def half_of(block, axis, upper):
    size = block.shape[axis] // 2
    low = lax.slice_in_dim(block, 0, size, axis=axis)
    high = lax.slice_in_dim(block, size, 2 * size, axis=axis)
    return jnp.where(upper, high, low)


def part_of(block, axis, index, parts):
    step = parts // 2
    while step:
        block = half_of(block, axis, bit_of(index, step))
        step //= 2
    return block


def matmul(left, right, contract):
    return lax.dot_general(
        left, right, (contract, ((), ())), preferred_element_type=jnp.float32
    )


CHUNKS = 4


def prepare_kernel(replicas, counts, src_degree, dst_degree, *refs):
    outs, (count_part, src_part, dst_part, sems) = refs[:replicas], refs[replicas:]
    src_rows, rows = outs[0].shape
    piece = src_rows // CHUNKS
    replica = lax.axis_index("rep")
    owners = [replica ^ step for step in range(1, replicas)] + [replica]
    degrees = [
        pltpu.make_async_copy(src_degree, src_part, sems.at[0]),
        pltpu.make_async_copy(dst_degree, dst_part, sems.at[1]),
    ]
    for copy in degrees:
        copy.start()
    copies = []
    for slot, owner in enumerate(owners):
        columns = pl.ds(pl.multiple_of(owner * rows, 128), rows)
        for chunk in range(CHUNKS):
            at = pl.ds(chunk * piece, piece)
            copy = pltpu.make_async_copy(
                counts.at[at, columns], count_part.at[slot, at], sems.at[2 + slot * CHUNKS + chunk]
            )
            copy.start()
            copies.append(copy)
    for copy in degrees:
        copy.wait()
    src_row = lax.rsqrt(src_part[...].astype(jnp.float32)).reshape(1, src_rows)
    square = (src_rows, src_rows)
    diagonal = lax.broadcasted_iota(jnp.int32, square, 0) == lax.broadcasted_iota(jnp.int32, square, 1)
    src_column = jnp.sum(
        jnp.where(diagonal, jnp.broadcast_to(src_row, square), 0.0), axis=1, keepdims=True
    )
    for slot, owner in enumerate(owners):
        pieces = [dst_part[at * rows : (at + 1) * rows] for at in range(replicas)]
        bit = 1
        while len(pieces) > 1:
            upper = bit_of(owner, bit)
            pieces = [jnp.where(upper, b, a) for a, b in zip(pieces[0::2], pieces[1::2])]
            bit *= 2
        dst_row = lax.rsqrt(pieces[0].astype(jnp.float32)).reshape(1, rows)
        for chunk in range(CHUNKS):
            at = slice(chunk * piece, (chunk + 1) * piece)
            copies[slot * CHUNKS + chunk].wait()
            values = count_part[slot, at, :].astype(jnp.float32)
            outs[slot][at, :] = (values * src_column[at] * dst_row).astype(jnp.bfloat16)


def prepare(counts, src_degree, dst_degree, replicas, rows):
    src_rows = counts.shape[0]
    return pl.pallas_call(
        functools.partial(prepare_kernel, replicas),
        out_shape=[pltpu.VMEM((src_rows, rows), jnp.bfloat16)] * replicas,
        in_specs=[pl.BlockSpec(memory_space=pl.ANY)] * 3,
        out_specs=[pl.BlockSpec(memory_space=pltpu.VMEM)] * replicas,
        scratch_shapes=[
            pltpu.VMEM((replicas, src_rows, rows), jnp.int32),
            pltpu.VMEM(src_degree.shape, jnp.int32),
            pltpu.VMEM(dst_degree.shape, jnp.int32),
            pltpu.SemaphoreType.DMA((2 + CHUNKS * replicas,)),
        ],
    )(counts, src_degree, dst_degree)


def own_kernel(own, inputs, term):
    term[...] = jnp.dot(own[...], inputs[...], preferred_element_type=jnp.float32)


def own_product(own, inputs):
    (src_rows, rows), width = own.shape, inputs.shape[1]
    return pl.pallas_call(
        own_kernel,
        out_shape=pltpu.VMEM((src_rows, width), jnp.float32),
        in_specs=[pl.BlockSpec(memory_space=pltpu.VMEM)] * 2,
        out_specs=pl.BlockSpec(memory_space=pltpu.VMEM),
        cost_estimate=pl.CostEstimate(
            flops=2 * src_rows * rows * width,
            bytes_accessed=2 * rows * (src_rows + width),
            transcendentals=0,
        ),
    )(*[pltpu.with_memory_space_constraint(block, pltpu.VMEM) for block in (own, inputs)])


def body(adjoint, active, counts, src_degree, dst_degree, inputs, weight):
    groups, replicas = lax.axis_size("grp"), lax.axis_size("rep")
    group, replica = lax.axis_index("grp"), lax.axis_index("rep")
    rows, width = inputs.shape
    block_rows = adjoint.shape[0]
    odd = bit_of(group, 1)
    fold = group ^ replica
    shift = 1 << groups.bit_length().bit_length()
    while shift:
        fold ^= fold >> shift
        shift //= 2
    upper_half = bit_of(fold, 1)

    *sent, own = prepare(counts, src_degree, dst_degree, replicas, rows)
    answers = [swap(part, "rep", step) for step, part in enumerate(sent, 1)]

    own_term = own_product(own, inputs)
    masked = (adjoint.astype(jnp.float32) * active.astype(jnp.float32)).astype(jnp.bfloat16)

    far = groups // 2
    others = [far >> at for at in range(1, far.bit_length() - 1)]
    far_steps = [far] * (far > 1)
    sum_steps = list(zip(others + far_steps, others[1:] + far_steps + others[:1]))
    row_steps = far_steps + others[-1:] + others[:-1]

    def gathered(mine, theirs, step):
        upper = bit_of(group, step)
        return in_order(upper, mine[:, None], theirs[:, None], 1).reshape(-1, block_rows, width)

    def arranged(mine):
        split = mine.reshape([2] * len(row_steps) + [block_rows, width])
        order = [row_steps.index(step) for step in far_steps + others]
        return split.transpose(order + [len(order), len(order) + 1]).reshape(-1, width)

    mine = masked.reshape(1, block_rows, width)
    left = list(row_steps)
    moving = None
    if left:
        moving = left.pop(0)
        theirs = swap(mine, "grp", moving)
    answers, own_term = lax.optimization_barrier((answers, own_term))
    parts = [own] + answers
    terms = [own_term] + [matmul(part, inputs, ((1,), (0,))) for part in answers]

    def ordered(pieces):
        step = 1
        while len(pieces) > 1:
            upper = bit_of(replica, step)
            pieces = [in_order(upper, a, b, 0) for a, b in zip(pieces[0::2], pieces[1::2])]
            step *= 2
        return pieces[0]

    def halves(block):
        pairs = block.reshape(groups // 2, 2, block_rows, block.shape[1])
        even = pairs[:, 0].reshape(-1, block.shape[1])
        uneven = pairs[:, 1].reshape(-1, block.shape[1])
        return even, uneven

    def chosen(upper, pair):
        return jnp.where(upper, pair[1], pair[0])

    terms = halves(ordered(terms))
    kept, sent = chosen(upper_half, terms), chosen(~upper_half, terms)
    total = kept + swap(sent.astype(jnp.bfloat16), "grp", 1).astype(jnp.float32)

    if moving:
        total, theirs = lax.optimization_barrier((total, theirs))
        mine, moving = gathered(mine, theirs, moving), None

    step = replicas // 2
    while step:
        upper = bit_of(replica, step)
        sent = half_of(total, 1, ~upper).astype(jnp.bfloat16)
        if step == 1 and left:
            sent, mine = lax.optimization_barrier((sent, mine))
            moving = left.pop(0)
            row_theirs = swap(mine, "grp", moving)
        theirs = crossed(sent, (0, 0), step)
        total = half_of(total, 1, upper) + theirs.astype(jnp.float32)
        step //= 2

    for at, steps in enumerate(sum_steps):
        sent = total.astype(jnp.bfloat16)
        answer = crossed(sent, steps, 0)
        if moving:
            sent, row_theirs = lax.optimization_barrier((sent, row_theirs))
            mine, moving = gathered(mine, row_theirs, moving), None
        if left and at:
            moving = left.pop(0)
            row_theirs = swap(mine, "grp", moving)
        if at == len(sum_steps) - 1:
            mine = arranged(mine)
            theirs = swap(mine, "grp", 1)
            scaled = halves(ordered(parts))
            grad_pre = matmul(chosen(odd, scaled), mine, ((0,), (0,)))
            grad_pre += matmul(chosen(~odd, scaled), theirs, ((0,), (0,)))
            grad_input = matmul(grad_pre.astype(jnp.bfloat16), weight, ((1,), (1,)))
            answer, grad_input = lax.optimization_barrier((answer, grad_input.astype(jnp.bfloat16)))
        total = sent.astype(jnp.float32) + answer.astype(jnp.float32)

    total = total.astype(jnp.bfloat16)
    other = swap(total, "grp", 1)
    vertex_total = rows * groups * replicas
    rows_of = jnp.where(odd ^ upper_half, theirs, mine), jnp.where(odd ^ upper_half, mine, theirs)
    grad_weight = matmul(total, rows_of[0], ((0,), (0,))) + matmul(other, rows_of[1], ((0,), (0,)))
    return (grad_input, grad_weight / vertex_total)


def solution(mesh):
    in_specs = (
        P("grp", None),
        P("grp", None),
        P("rep", "grp"),
        P("rep"),
        P("grp"),
        P(("grp", "rep"), None),
        P(),
    )
    out_specs = (P(("grp", "rep"), None), P("rep", None))
    return jax.shard_map(body, mesh=mesh, in_specs=in_specs, out_specs=out_specs, check_vma=False)
```

```python
import functools

import jax
import jax.numpy as jnp
from jax import lax
from jax.experimental import pallas as pl
from jax.experimental.pallas import tpu as pltpu
from jax.sharding import PartitionSpec as P


def swap(block, axis, step):
    size = lax.axis_size(axis)
    return lax.ppermute(block, axis, [(at, at ^ step) for at in range(size)])


def parity(number):
    count = 0
    while number:
        count ^= number & 1
        number >>= 1
    return count


def crossed(block, group_steps, replica_step):
    groups, replicas = lax.axis_size("grp"), lax.axis_size("rep")
    pairs = []
    for group in range(groups):
        for replica in range(replicas):
            step = group_steps[parity(group) ^ parity(replica)] | 1
            pairs.append((group * replicas + replica, (group ^ step) * replicas + (replica ^ replica_step)))
    return lax.ppermute(block, ("grp", "rep"), pairs)


def bit_of(index, step):
    return (index & step) != 0


def in_order(upper, mine, theirs, axis):
    return jnp.where(
        upper,
        jnp.concatenate([theirs, mine], axis),
        jnp.concatenate([mine, theirs], axis),
    )


def half_of(block, axis, upper):
    size = block.shape[axis] // 2
    low = lax.slice_in_dim(block, 0, size, axis=axis)
    high = lax.slice_in_dim(block, size, 2 * size, axis=axis)
    return jnp.where(upper, high, low)


def part_of(block, axis, index, parts):
    step = parts // 2
    while step:
        block = half_of(block, axis, bit_of(index, step))
        step //= 2
    return block


def matmul(left, right, contract):
    return lax.dot_general(
        left, right, (contract, ((), ())), preferred_element_type=jnp.float32
    )


CHUNKS = 4


def prepare_kernel(replicas, counts, src_degree, dst_degree, *refs):
    outs, (count_part, src_part, dst_part, sems) = refs[:replicas], refs[replicas:]
    src_rows, rows = outs[0].shape
    piece = src_rows // CHUNKS
    replica = lax.axis_index("rep")
    owners = [replica ^ step for step in range(1, replicas)] + [replica]
    degrees = [
        pltpu.make_async_copy(src_degree, src_part, sems.at[0]),
        pltpu.make_async_copy(dst_degree, dst_part, sems.at[1]),
    ]
    for copy in degrees:
        copy.start()
    copies = []
    for slot, owner in enumerate(owners):
        columns = pl.ds(pl.multiple_of(owner * rows, 128), rows)
        for chunk in range(CHUNKS):
            at = pl.ds(chunk * piece, piece)
            copy = pltpu.make_async_copy(
                counts.at[at, columns], count_part.at[slot, at], sems.at[2 + slot * CHUNKS + chunk]
            )
            copy.start()
            copies.append(copy)
    for copy in degrees:
        copy.wait()
    src_row = lax.rsqrt(src_part[...].astype(jnp.float32)).reshape(1, src_rows)
    square = (src_rows, src_rows)
    diagonal = lax.broadcasted_iota(jnp.int32, square, 0) == lax.broadcasted_iota(jnp.int32, square, 1)
    src_column = jnp.sum(
        jnp.where(diagonal, jnp.broadcast_to(src_row, square), 0.0), axis=1, keepdims=True
    )
    for slot, owner in enumerate(owners):
        pieces = [dst_part[at * rows : (at + 1) * rows] for at in range(replicas)]
        bit = 1
        while len(pieces) > 1:
            upper = bit_of(owner, bit)
            pieces = [jnp.where(upper, b, a) for a, b in zip(pieces[0::2], pieces[1::2])]
            bit *= 2
        dst_row = lax.rsqrt(pieces[0].astype(jnp.float32)).reshape(1, rows)
        for chunk in range(CHUNKS):
            at = slice(chunk * piece, (chunk + 1) * piece)
            copies[slot * CHUNKS + chunk].wait()
            values = count_part[slot, at, :].astype(jnp.float32)
            outs[slot][at, :] = (values * src_column[at] * dst_row).astype(jnp.bfloat16)


def prepare(counts, src_degree, dst_degree, replicas, rows):
    src_rows = counts.shape[0]
    return pl.pallas_call(
        functools.partial(prepare_kernel, replicas),
        out_shape=[pltpu.VMEM((src_rows, rows), jnp.bfloat16)] * replicas,
        in_specs=[pl.BlockSpec(memory_space=pl.ANY)] * 3,
        out_specs=[pl.BlockSpec(memory_space=pltpu.VMEM)] * replicas,
        scratch_shapes=[
            pltpu.VMEM((replicas, src_rows, rows), jnp.int32),
            pltpu.VMEM(src_degree.shape, jnp.int32),
            pltpu.VMEM(dst_degree.shape, jnp.int32),
            pltpu.SemaphoreType.DMA((2 + CHUNKS * replicas,)),
        ],
    )(counts, src_degree, dst_degree)


def own_kernel(own, inputs, term):
    term[...] = jnp.dot(own[...], inputs[...], preferred_element_type=jnp.float32)


def own_product(own, inputs):
    (src_rows, rows), width = own.shape, inputs.shape[1]
    return pl.pallas_call(
        own_kernel,
        out_shape=pltpu.VMEM((src_rows, width), jnp.float32),
        in_specs=[pl.BlockSpec(memory_space=pltpu.VMEM)] * 2,
        out_specs=pl.BlockSpec(memory_space=pltpu.VMEM),
        cost_estimate=pl.CostEstimate(
            flops=2 * src_rows * rows * width,
            bytes_accessed=2 * rows * (src_rows + width),
            transcendentals=0,
        ),
    )(*[pltpu.with_memory_space_constraint(block, pltpu.VMEM) for block in (own, inputs)])


def final_kernel(scale, mine, other, rows, out, parts, sems):
    count, cols, _ = parts.shape
    copies = []
    for at in range(count):
        piece = slice(at * cols, (at + 1) * cols)
        product = matmul(other[:, piece], rows[...], ((0,), (0,)))
        parts[at] = (mine[piece, :] + product) * scale
        copies.append(pltpu.make_async_copy(parts.at[at], out.at[piece, :], sems.at[at]))
        copies[at].start()
    for copy in copies:
        copy.wait()


def final_product(mine, other, rows, scale):
    cols = min(other.shape[1], 128)
    count = other.shape[1] // cols
    return pl.pallas_call(
        functools.partial(final_kernel, scale),
        out_shape=jax.ShapeDtypeStruct(mine.shape, jnp.float32),
        in_specs=[pl.BlockSpec(memory_space=pltpu.VMEM)] * 3,
        out_specs=pl.BlockSpec(memory_space=pl.ANY),
        scratch_shapes=[
            pltpu.VMEM((count, cols, mine.shape[1]), jnp.float32),
            pltpu.SemaphoreType.DMA((count,)),
        ],
    )(*[pltpu.with_memory_space_constraint(block, pltpu.VMEM) for block in (mine, other, rows)])


def body(adjoint, active, counts, src_degree, dst_degree, inputs, weight):
    groups, replicas = lax.axis_size("grp"), lax.axis_size("rep")
    group, replica = lax.axis_index("grp"), lax.axis_index("rep")
    rows, width = inputs.shape
    block_rows = adjoint.shape[0]
    odd = bit_of(group, 1)
    fold = group ^ replica
    shift = 1 << groups.bit_length().bit_length()
    while shift:
        fold ^= fold >> shift
        shift //= 2
    upper_half = bit_of(fold, 1)

    *sent, own = prepare(counts, src_degree, dst_degree, replicas, rows)
    answers = [swap(part, "rep", step) for step, part in enumerate(sent, 1)]

    own_term = own_product(own, inputs)
    masked = (adjoint.astype(jnp.float32) * active.astype(jnp.float32)).astype(jnp.bfloat16)

    far = groups // 2
    others = [far >> at for at in range(1, far.bit_length() - 1)]
    far_steps = [far] * (far > 1)
    sum_steps = list(zip(others + far_steps, others[1:] + far_steps + others[:1]))
    row_steps = far_steps + others[-1:] + others[:-1]

    def gathered(mine, theirs, step):
        upper = bit_of(group, step)
        return in_order(upper, mine[:, None], theirs[:, None], 1).reshape(-1, block_rows, width)

    def arranged(mine):
        split = mine.reshape([2] * len(row_steps) + [block_rows, width])
        order = [row_steps.index(step) for step in far_steps + others]
        return split.transpose(order + [len(order), len(order) + 1]).reshape(-1, width)

    mine = masked.reshape(1, block_rows, width)
    left = list(row_steps)
    moving = None
    if left:
        moving = left.pop(0)
        theirs = swap(mine, "grp", moving)
    answers, own_term = lax.optimization_barrier((answers, own_term))
    parts = [own] + answers
    terms = [own_term] + [matmul(part, inputs, ((1,), (0,))) for part in answers]

    def ordered(pieces):
        step = 1
        while len(pieces) > 1:
            upper = bit_of(replica, step)
            pieces = [in_order(upper, a, b, 0) for a, b in zip(pieces[0::2], pieces[1::2])]
            step *= 2
        return pieces[0]

    def halves(block):
        pairs = block.reshape(groups // 2, 2, block_rows, block.shape[1])
        even = pairs[:, 0].reshape(-1, block.shape[1])
        uneven = pairs[:, 1].reshape(-1, block.shape[1])
        return even, uneven

    def chosen(upper, pair):
        return jnp.where(upper, pair[1], pair[0])

    terms = halves(ordered(terms))
    kept, sent = chosen(upper_half, terms), chosen(~upper_half, terms)
    total = kept + swap(sent.astype(jnp.bfloat16), "grp", 1).astype(jnp.float32)

    if moving:
        total, theirs = lax.optimization_barrier((total, theirs))
        mine, moving = gathered(mine, theirs, moving), None

    step = replicas // 2
    while step:
        upper = bit_of(replica, step)
        sent = half_of(total, 1, ~upper).astype(jnp.bfloat16)
        if step == 1 and left:
            sent, mine = lax.optimization_barrier((sent, mine))
            moving = left.pop(0)
            row_theirs = swap(mine, "grp", moving)
        theirs = crossed(sent, (0, 0), step)
        total = half_of(total, 1, upper) + theirs.astype(jnp.float32)
        step //= 2

    theirs = None
    for at, steps in enumerate(sum_steps):
        sent = total.astype(jnp.bfloat16)
        answer = crossed(sent, steps, 0)
        if moving:
            sent, row_theirs = lax.optimization_barrier((sent, row_theirs))
            mine, moving = gathered(mine, row_theirs, moving), None
        if left:
            moving = left.pop(0)
            row_theirs = swap(mine, "grp", moving)
        elif theirs is None:
            mine = arranged(mine)
            theirs = swap(mine, "grp", 1)
            if at < len(sum_steps) - 1:
                answer, mine = lax.optimization_barrier((answer, mine))
        if at == len(sum_steps) - 1:
            scaled = halves(ordered(parts))
            grad_pre = matmul(chosen(odd, scaled), mine, ((0,), (0,)))
            grad_pre += matmul(chosen(~odd, scaled), theirs, ((0,), (0,)))
            grad_input = matmul(grad_pre.astype(jnp.bfloat16), weight, ((1,), (1,)))
            answer, grad_input = lax.optimization_barrier((answer, grad_input.astype(jnp.bfloat16)))
        total = sent.astype(jnp.float32) + answer.astype(jnp.float32)

    total = total.astype(jnp.bfloat16)
    other = swap(total, "grp", 1)
    vertex_total = rows * groups * replicas
    swapped = odd ^ upper_half
    product = matmul(total, jnp.where(swapped, theirs, mine), ((0,), (0,)))
    rest = jnp.where(swapped, mine, theirs)
    other, product, rest = lax.optimization_barrier((other, product, rest))
    return (grad_input, final_product(product, other, rest, 1.0 / vertex_total))


def solution(mesh):
    in_specs = (
        P("grp", None),
        P("grp", None),
        P("rep", "grp"),
        P("rep"),
        P("grp"),
        P(("grp", "rep"), None),
        P(),
    )
    out_specs = (P(("grp", "rep"), None), P("rep", None))
    return jax.shard_map(body, mesh=mesh, in_specs=in_specs, out_specs=out_specs, check_vma=False)
```

```python
import functools

import jax
import jax.numpy as jnp
from jax import lax
from jax.experimental import pallas as pl
from jax.experimental.pallas import tpu as pltpu
from jax.sharding import PartitionSpec as P


def swap(block, axis, step):
    size = lax.axis_size(axis)
    return lax.ppermute(block, axis, [(at, at ^ step) for at in range(size)])


def parity(number):
    count = 0
    while number:
        count ^= number & 1
        number >>= 1
    return count


def crossed(block, group_steps, replica_step):
    groups, replicas = lax.axis_size("grp"), lax.axis_size("rep")
    pairs = []
    for group in range(groups):
        for replica in range(replicas):
            step = group_steps[parity(group) ^ parity(replica)] | 1
            pairs.append((group * replicas + replica, (group ^ step) * replicas + (replica ^ replica_step)))
    return lax.ppermute(block, ("grp", "rep"), pairs)


def bit_of(index, step):
    return (index & step) != 0


def in_order(upper, mine, theirs, axis):
    return jnp.where(
        upper,
        jnp.concatenate([theirs, mine], axis),
        jnp.concatenate([mine, theirs], axis),
    )


def half_of(block, axis, upper):
    size = block.shape[axis] // 2
    low = lax.slice_in_dim(block, 0, size, axis=axis)
    high = lax.slice_in_dim(block, size, 2 * size, axis=axis)
    return jnp.where(upper, high, low)


def part_of(block, axis, index, parts):
    step = parts // 2
    while step:
        block = half_of(block, axis, bit_of(index, step))
        step //= 2
    return block


def add(first, second):
    return second if first is None else first if second is None else first + second


def matmul(left, right, contract):
    return lax.dot_general(
        left, right, (contract, ((), ())), preferred_element_type=jnp.float32
    )


CHUNKS = 4


def prepare_kernel(counts, src_degree, dst_degree, adjoint, active, *refs):
    outs, masked, scratch = refs[:-7], refs[-7], refs[-6:]
    count_part, src_part, dst_part, adjoint_part, active_part, sems = scratch
    src_rows, rows = outs[0].shape
    piece = src_rows // CHUNKS
    replicas = len(outs)
    replica = lax.axis_index("rep")
    owners = [replica ^ step for step in range(1, replicas)] + [replica]
    degrees = [
        pltpu.make_async_copy(src_degree, src_part, sems.at[0]),
        pltpu.make_async_copy(dst_degree, dst_part, sems.at[1]),
    ]
    factors = [
        pltpu.make_async_copy(adjoint, adjoint_part, sems.at[2]),
        pltpu.make_async_copy(active, active_part, sems.at[3]),
    ]
    copies = []
    for slot, owner in enumerate(owners):
        columns = pl.ds(pl.multiple_of(owner * rows, 128), rows)
        for chunk in range(CHUNKS):
            at = pl.ds(chunk * piece, piece)
            copies.append(
                pltpu.make_async_copy(
                    counts.at[at, columns],
                    count_part.at[slot, at],
                    sems.at[4 + slot * CHUNKS + chunk],
                )
            )
    for copy in degrees + copies + factors:
        copy.start()
    for copy in degrees:
        copy.wait()
    src_row = lax.rsqrt(src_part[...].astype(jnp.float32)).reshape(1, src_rows)
    square = (src_rows, src_rows)
    diagonal = lax.broadcasted_iota(jnp.int32, square, 0) == lax.broadcasted_iota(jnp.int32, square, 1)
    src_column = jnp.sum(
        jnp.where(diagonal, jnp.broadcast_to(src_row, square), 0.0), axis=1, keepdims=True
    )
    for slot, owner in enumerate(owners):
        pieces = [dst_part[at * rows : (at + 1) * rows] for at in range(replicas)]
        bit = 1
        while len(pieces) > 1:
            upper = bit_of(owner, bit)
            pieces = [jnp.where(upper, b, a) for a, b in zip(pieces[0::2], pieces[1::2])]
            bit *= 2
        dst_row = lax.rsqrt(pieces[0].astype(jnp.float32)).reshape(1, rows)
        for chunk in range(CHUNKS):
            at = slice(chunk * piece, (chunk + 1) * piece)
            copies[slot * CHUNKS + chunk].wait()
            values = count_part[slot, at, :].astype(jnp.float32)
            outs[slot][at, :] = (values * src_column[at] * dst_row).astype(jnp.bfloat16)
    for copy in factors:
        copy.wait()
    values = adjoint_part[...].astype(jnp.float32) * active_part[...].astype(jnp.float32)
    masked[...] = values.astype(jnp.bfloat16)


def prepare(counts, src_degree, dst_degree, adjoint, active, replicas, rows):
    src_rows = counts.shape[0]
    return pl.pallas_call(
        prepare_kernel,
        out_shape=[pltpu.VMEM((src_rows, rows), jnp.bfloat16)] * replicas
        + [pltpu.VMEM(adjoint.shape, jnp.bfloat16)],
        in_specs=[pl.BlockSpec(memory_space=pl.ANY)] * 5,
        out_specs=[pl.BlockSpec(memory_space=pltpu.VMEM)] * (replicas + 1),
        scratch_shapes=[
            pltpu.VMEM((replicas, src_rows, rows), jnp.int32),
            pltpu.VMEM(src_degree.shape, jnp.int32),
            pltpu.VMEM(dst_degree.shape, jnp.int32),
            pltpu.VMEM(adjoint.shape, adjoint.dtype),
            pltpu.VMEM(active.shape, active.dtype),
            pltpu.SemaphoreType.DMA((4 + CHUNKS * replicas,)),
        ],
    )(counts, src_degree, dst_degree, adjoint, active)


def own_kernel(own, inputs, term):
    term[...] = jnp.dot(own[...], inputs[...], preferred_element_type=jnp.float32)


def own_product(own, inputs):
    (src_rows, rows), width = own.shape, inputs.shape[1]
    return pl.pallas_call(
        own_kernel,
        out_shape=pltpu.VMEM((src_rows, width), jnp.float32),
        in_specs=[pl.BlockSpec(memory_space=pltpu.VMEM)] * 2,
        out_specs=pl.BlockSpec(memory_space=pltpu.VMEM),
        cost_estimate=pl.CostEstimate(
            flops=2 * src_rows * rows * width,
            bytes_accessed=2 * rows * (src_rows + width),
            transcendentals=0,
        ),
    )(*[pltpu.with_memory_space_constraint(block, pltpu.VMEM) for block in (own, inputs)])


def final_kernel(scale, mine, other, rows, out, parts, sems):
    count, cols, _ = parts.shape
    copies = []
    for at in range(count):
        piece = slice(at * cols, (at + 1) * cols)
        product = matmul(other[:, piece], rows[...], ((0,), (0,)))
        parts[at] = (mine[piece, :] + product) * scale
        copies.append(pltpu.make_async_copy(parts.at[at], out.at[piece, :], sems.at[at]))
        copies[at].start()
    for copy in copies:
        copy.wait()


def final_product(mine, other, rows, scale):
    cols = min(other.shape[1], 128)
    count = other.shape[1] // cols
    return pl.pallas_call(
        functools.partial(final_kernel, scale),
        out_shape=jax.ShapeDtypeStruct(mine.shape, jnp.float32),
        in_specs=[pl.BlockSpec(memory_space=pltpu.VMEM)] * 3,
        out_specs=pl.BlockSpec(memory_space=pl.ANY),
        scratch_shapes=[
            pltpu.VMEM((count, cols, mine.shape[1]), jnp.float32),
            pltpu.SemaphoreType.DMA((count,)),
        ],
    )(*[pltpu.with_memory_space_constraint(block, pltpu.VMEM) for block in (mine, other, rows)])


def body(adjoint, active, counts, src_degree, dst_degree, inputs, weight):
    groups, replicas = lax.axis_size("grp"), lax.axis_size("rep")
    group, replica = lax.axis_index("grp"), lax.axis_index("rep")
    rows, width = inputs.shape
    block_rows = adjoint.shape[0]
    odd = bit_of(group, 1)
    fold = group ^ replica
    shift = 1 << groups.bit_length().bit_length()
    while shift:
        fold ^= fold >> shift
        shift //= 2
    upper_half = bit_of(fold, 1)

    *sent, own, masked = prepare(
        counts, src_degree, dst_degree, adjoint, active, replicas, rows
    )
    answers = [swap(part, "rep", step) for step, part in enumerate(sent, 1)]

    own_term = own_product(own, inputs)

    far = groups // 2
    others = [far >> at for at in range(1, far.bit_length() - 1)]
    far_steps = [far] * (far > 1)
    sum_steps = list(zip(others + far_steps, others[1:] + far_steps + others[:1]))
    row_steps = far_steps + others[-1:] + others[:-1]

    def gathered(mine, theirs, step):
        upper = bit_of(group, step)
        return in_order(upper, mine[:, None], theirs[:, None], 1).reshape(-1, block_rows, width)

    def arranged(mine):
        split = mine.reshape([2] * len(row_steps) + [block_rows, width])
        order = [row_steps.index(step) for step in far_steps + others]
        return split.transpose(order + [len(order), len(order) + 1]).reshape(-1, width)

    mine = masked.reshape(1, block_rows, width)
    left = list(row_steps)
    moving = None
    if left:
        moving = left.pop(0)
        theirs = swap(mine, "grp", moving)
    parts = [own] + answers

    def ordered(pieces):
        step = 1
        while len(pieces) > 1:
            upper = bit_of(replica, step)
            pieces = [in_order(upper, a, b, 0) for a, b in zip(pieces[0::2], pieces[1::2])]
            step *= 2
        return pieces[0]

    def halves(block):
        pairs = block.reshape(-1, 2, block_rows, block.shape[1])
        even = pairs[:, 0].reshape(-1, block.shape[1])
        uneven = pairs[:, 1].reshape(-1, block.shape[1])
        return even, uneven

    def chosen(upper, pair):
        return jnp.where(upper, pair[1], pair[0])

    def neighbour_sum(block):
        pair = halves(block)
        kept, sent = chosen(upper_half, pair), chosen(~upper_half, pair)
        return kept + swap(sent.astype(jnp.bfloat16), "grp", 1).astype(jnp.float32)

    own_sum = neighbour_sum(own_term)
    early = [part_of(own_sum, 1, replica, replicas)]
    leaving = [
        part_of(own_sum, 1, replica ^ step, replicas).astype(jnp.bfloat16)
        for step in range(1, replicas)
    ]
    answers, early = lax.optimization_barrier((answers, early))
    early_theirs = [crossed(block, (0, 0), step) for step, block in enumerate(leaving, 1)]

    terms = neighbour_sum(jnp.concatenate([matmul(part, inputs, ((1,), (0,))) for part in answers], 0))
    pieces = [None] + jnp.split(terms, replicas - 1, axis=0)
    if moving:
        pieces, theirs = lax.optimization_barrier((pieces, theirs))
        mine, moving = gathered(mine, theirs, moving), None

    step = replicas // 2
    while step:
        upper = bit_of(replica, step)
        there = [at for at, piece in enumerate(pieces) if piece is not None]
        sent = jnp.concatenate([half_of(pieces[at], 1, ~upper) for at in there], 0).astype(jnp.bfloat16)
        if step == 1 and left:
            sent, mine = lax.optimization_barrier((sent, mine))
            moving = left.pop(0)
            row_theirs = swap(mine, "grp", moving)
        theirs = jnp.split(crossed(sent, (0, 0), step).astype(jnp.float32), len(there), axis=0)
        pieces = [piece if piece is None else half_of(piece, 1, upper) for piece in pieces]
        if step == 1:
            kept = [pieces[at] for at in there]
            kept, early_theirs = lax.optimization_barrier((kept, early_theirs))
            for at, piece in zip(there, kept):
                pieces[at] = piece
        for at, block in zip(there, theirs):
            pieces[at ^ step] = add(pieces[at ^ step], block)
        step //= 2
    early += [block.astype(jnp.float32) for block in early_theirs]
    total = ordered([add(*pair) for pair in zip(pieces, early)])

    theirs = None
    for at, steps in enumerate(sum_steps):
        sent = total.astype(jnp.bfloat16)
        answer = crossed(sent, steps, 0)
        if moving:
            sent, row_theirs = lax.optimization_barrier((sent, row_theirs))
            mine, moving = gathered(mine, row_theirs, moving), None
        if left:
            moving = left.pop(0)
            row_theirs = swap(mine, "grp", moving)
        elif theirs is None:
            mine = arranged(mine)
            theirs = swap(mine, "grp", 1)
            if at < len(sum_steps) - 1:
                answer, mine = lax.optimization_barrier((answer, mine))
        if at == len(sum_steps) - 1:
            scaled = halves(ordered(parts))
            grad_pre = matmul(chosen(odd, scaled), mine, ((0,), (0,)))
            grad_pre += matmul(chosen(~odd, scaled), theirs, ((0,), (0,)))
            grad_input = matmul(grad_pre.astype(jnp.bfloat16), weight, ((1,), (1,)))
            answer, grad_input = lax.optimization_barrier((answer, grad_input.astype(jnp.bfloat16)))
        total = sent.astype(jnp.float32) + answer.astype(jnp.float32)

    total = total.astype(jnp.bfloat16)
    other = swap(total, "grp", 1)
    vertex_total = rows * groups * replicas
    swapped = odd ^ upper_half
    product = matmul(total, jnp.where(swapped, theirs, mine), ((0,), (0,)))
    rest = jnp.where(swapped, mine, theirs)
    other, product, rest = lax.optimization_barrier((other, product, rest))
    return (grad_input, final_product(product, other, rest, 1.0 / vertex_total))


def solution(mesh):
    in_specs = (
        P("grp", None),
        P("grp", None),
        P("rep", "grp"),
        P("rep"),
        P("grp"),
        P(("grp", "rep"), None),
        P(),
    )
    out_specs = (P(("grp", "rep"), None), P("rep", None))
    return jax.shard_map(body, mesh=mesh, in_specs=in_specs, out_specs=out_specs, check_vma=False)
```

```python
import functools

import jax
import jax.numpy as jnp
from jax import lax
from jax.experimental import pallas as pl
from jax.experimental.pallas import tpu as pltpu
from jax.sharding import PartitionSpec as P


def swap(block, axis, step):
    size = lax.axis_size(axis)
    return lax.ppermute(block, axis, [(at, at ^ step) for at in range(size)])


def parity(number):
    count = 0
    while number:
        count ^= number & 1
        number >>= 1
    return count


def crossed(block, group_steps, replica_step):
    groups, replicas = lax.axis_size("grp"), lax.axis_size("rep")
    pairs = []
    for group in range(groups):
        for replica in range(replicas):
            step = group_steps[parity(group) ^ parity(replica)] | 1
            pairs.append((group * replicas + replica, (group ^ step) * replicas + (replica ^ replica_step)))
    return lax.ppermute(block, ("grp", "rep"), pairs)


def bit_of(index, step):
    return (index & step) != 0


def in_order(upper, mine, theirs, axis):
    return jnp.where(
        upper,
        jnp.concatenate([theirs, mine], axis),
        jnp.concatenate([mine, theirs], axis),
    )


def half_of(block, axis, upper):
    size = block.shape[axis] // 2
    low = lax.slice_in_dim(block, 0, size, axis=axis)
    high = lax.slice_in_dim(block, size, 2 * size, axis=axis)
    return jnp.where(upper, high, low)


def part_of(block, axis, index, parts):
    step = parts // 2
    while step:
        block = half_of(block, axis, bit_of(index, step))
        step //= 2
    return block


def add(first, second):
    return second if first is None else first if second is None else first + second


def matmul(left, right, contract):
    return lax.dot_general(
        left, right, (contract, ((), ())), preferred_element_type=jnp.float32
    )


CHUNKS = 4


def prepare_kernel(counts, src_degree, dst_degree, adjoint, active, *refs):
    outs, (src_scale, dst_scale, masked), scratch = refs[:-9], refs[-9:-6], refs[-6:]
    count_part, src_part, dst_part, adjoint_part, active_part, sems = scratch
    src_rows, rows = outs[0].shape
    piece = src_rows // CHUNKS
    replicas = len(outs) + 1
    replica = lax.axis_index("rep")
    owners = [replica ^ step for step in range(1, replicas)]
    degrees = [
        pltpu.make_async_copy(src_degree, src_part, sems.at[0]),
        pltpu.make_async_copy(dst_degree, dst_part, sems.at[1]),
    ]
    factors = [
        pltpu.make_async_copy(adjoint, adjoint_part, sems.at[2]),
        pltpu.make_async_copy(active, active_part, sems.at[3]),
    ]
    copies = []
    for slot, owner in enumerate(owners):
        columns = pl.ds(pl.multiple_of(owner * rows, 128), rows)
        for chunk in range(CHUNKS):
            at = pl.ds(chunk * piece, piece)
            copies.append(
                pltpu.make_async_copy(
                    counts.at[at, columns],
                    count_part.at[slot, at],
                    sems.at[4 + slot * CHUNKS + chunk],
                )
            )
    for copy in degrees + copies + factors:
        copy.start()
    for copy in degrees:
        copy.wait()
    src_row = lax.rsqrt(src_part[...].astype(jnp.float32)).reshape(1, src_rows)
    square = (src_rows, src_rows)
    diagonal = lax.broadcasted_iota(jnp.int32, square, 0) == lax.broadcasted_iota(jnp.int32, square, 1)
    src_column = jnp.sum(
        jnp.where(diagonal, jnp.broadcast_to(src_row, square), 0.0), axis=1, keepdims=True
    )
    src_scale[...] = src_row
    for slot, owner in enumerate(owners + [replica]):
        pieces = [dst_part[at * rows : (at + 1) * rows] for at in range(replicas)]
        bit = 1
        while len(pieces) > 1:
            upper = bit_of(owner, bit)
            pieces = [jnp.where(upper, b, a) for a, b in zip(pieces[0::2], pieces[1::2])]
            bit *= 2
        dst_row = lax.rsqrt(pieces[0].astype(jnp.float32)).reshape(1, rows)
        if slot == len(outs):
            dst_scale[...] = dst_row
            break
        for chunk in range(CHUNKS):
            at = slice(chunk * piece, (chunk + 1) * piece)
            copies[slot * CHUNKS + chunk].wait()
            values = count_part[slot, at, :].astype(jnp.float32)
            outs[slot][at, :] = (values * src_column[at] * dst_row).astype(jnp.bfloat16)
    for copy in factors:
        copy.wait()
    values = adjoint_part[...].astype(jnp.float32) * active_part[...].astype(jnp.float32)
    masked[...] = values.astype(jnp.bfloat16)


def prepare(counts, src_degree, dst_degree, adjoint, active, replicas, rows):
    src_rows, others = counts.shape[0], replicas - 1
    return pl.pallas_call(
        prepare_kernel,
        out_shape=[pltpu.VMEM((src_rows, rows), jnp.bfloat16)] * others
        + [
            pltpu.VMEM((1, src_rows), jnp.float32),
            pltpu.VMEM((1, rows), jnp.float32),
            pltpu.VMEM(adjoint.shape, jnp.bfloat16),
        ],
        in_specs=[pl.BlockSpec(memory_space=pl.ANY)] * 5,
        out_specs=[pl.BlockSpec(memory_space=pltpu.VMEM)] * (others + 3),
        scratch_shapes=[
            pltpu.VMEM((others, src_rows, rows), jnp.int32),
            pltpu.VMEM(src_degree.shape, jnp.int32),
            pltpu.VMEM(dst_degree.shape, jnp.int32),
            pltpu.VMEM(adjoint.shape, adjoint.dtype),
            pltpu.VMEM(active.shape, active.dtype),
            pltpu.SemaphoreType.DMA((4 + CHUNKS * others,)),
        ],
    )(counts, src_degree, dst_degree, adjoint, active)


def own_kernel(own, inputs, term):
    term[...] = jnp.dot(own[...], inputs[...], preferred_element_type=jnp.float32)


def own_product(own, inputs):
    (src_rows, rows), width = own.shape, inputs.shape[1]
    return pl.pallas_call(
        own_kernel,
        out_shape=pltpu.VMEM((src_rows, width), jnp.float32),
        in_specs=[pl.BlockSpec(memory_space=pltpu.VMEM)] * 2,
        out_specs=pl.BlockSpec(memory_space=pltpu.VMEM),
        cost_estimate=pl.CostEstimate(
            flops=2 * src_rows * rows * width,
            bytes_accessed=2 * rows * (src_rows + width),
            transcendentals=0,
        ),
    )(*[pltpu.with_memory_space_constraint(block, pltpu.VMEM) for block in (own, inputs)])


def final_kernel(scale, mine, other, rows, out, parts, sems):
    count, cols, _ = parts.shape
    copies = []
    for at in range(count):
        piece = slice(at * cols, (at + 1) * cols)
        product = matmul(other[:, piece], rows[...], ((0,), (0,)))
        parts[at] = (mine[piece, :] + product) * scale
        copies.append(pltpu.make_async_copy(parts.at[at], out.at[piece, :], sems.at[at]))
        copies[at].start()
    for copy in copies:
        copy.wait()


def final_product(mine, other, rows, scale):
    cols = min(other.shape[1], 128)
    count = other.shape[1] // cols
    return pl.pallas_call(
        functools.partial(final_kernel, scale),
        out_shape=jax.ShapeDtypeStruct(mine.shape, jnp.float32),
        in_specs=[pl.BlockSpec(memory_space=pltpu.VMEM)] * 3,
        out_specs=pl.BlockSpec(memory_space=pl.ANY),
        scratch_shapes=[
            pltpu.VMEM((count, cols, mine.shape[1]), jnp.float32),
            pltpu.SemaphoreType.DMA((count,)),
        ],
    )(*[pltpu.with_memory_space_constraint(block, pltpu.VMEM) for block in (mine, other, rows)])


def body(adjoint, active, counts, src_degree, dst_degree, inputs, weight):
    groups, replicas = lax.axis_size("grp"), lax.axis_size("rep")
    group, replica = lax.axis_index("grp"), lax.axis_index("rep")
    rows, width = inputs.shape
    block_rows = adjoint.shape[0]
    odd = bit_of(group, 1)
    fold = group ^ replica
    shift = 1 << groups.bit_length().bit_length()
    while shift:
        fold ^= fold >> shift
        shift //= 2
    upper_half = bit_of(fold, 1)

    *sent, src_scale, dst_scale, masked = prepare(
        counts, src_degree, dst_degree, adjoint, active, replicas, rows
    )
    answers = [swap(part, "rep", step) for step, part in enumerate(sent, 1)]

    own = part_of(counts, 1, replica, replicas).astype(jnp.float32)
    own = (own * src_scale.reshape(-1, 1) * dst_scale).astype(jnp.bfloat16)
    own_term = own_product(own, inputs)

    far = groups // 2
    others = [far >> at for at in range(1, far.bit_length() - 1)]
    far_steps = [far] * (far > 1)
    sum_steps = list(zip(others + far_steps, others[1:] + far_steps + others[:1]))
    row_steps = far_steps + others

    def gathered(mine, theirs, step):
        upper = bit_of(group, step)
        return in_order(upper, mine[:, None], theirs[:, None], 1).reshape(-1, block_rows, width)

    def arranged(mine):
        split = mine.reshape([2] * len(row_steps) + [block_rows, width])
        order = [row_steps.index(step) for step in far_steps + others]
        return split.transpose(order + [len(order), len(order) + 1]).reshape(-1, width)

    mine = masked.reshape(1, block_rows, width)
    left = list(row_steps)
    moving = None
    if left:
        moving = left.pop(0)
        theirs = swap(mine, "grp", moving)
    parts = [own] + answers

    def ordered(pieces):
        step = 1
        while len(pieces) > 1:
            upper = bit_of(replica, step)
            pieces = [in_order(upper, a, b, 0) for a, b in zip(pieces[0::2], pieces[1::2])]
            step *= 2
        return pieces[0]

    def halves(block):
        pairs = block.reshape(-1, 2, block_rows, block.shape[1])
        even = pairs[:, 0].reshape(-1, block.shape[1])
        uneven = pairs[:, 1].reshape(-1, block.shape[1])
        return even, uneven

    def chosen(upper, pair):
        return jnp.where(upper, pair[1], pair[0])

    def neighbour_sum(block):
        pair = halves(block)
        kept, sent = chosen(upper_half, pair), chosen(~upper_half, pair)
        return kept + swap(sent.astype(jnp.bfloat16), "grp", 1).astype(jnp.float32)

    own_sum = neighbour_sum(own_term)
    early = [part_of(own_sum, 1, replica, replicas)]
    leaving = [
        part_of(own_sum, 1, replica ^ step, replicas).astype(jnp.bfloat16)
        for step in range(1, replicas)
    ]
    answers, early = lax.optimization_barrier((answers, early))
    early_theirs = [crossed(block, (0, 0), step) for step, block in enumerate(leaving, 1)]

    terms = neighbour_sum(jnp.concatenate([matmul(part, inputs, ((1,), (0,))) for part in answers], 0))
    pieces = [None] + jnp.split(terms, replicas - 1, axis=0)
    if moving:
        pieces, theirs = lax.optimization_barrier((pieces, theirs))
        mine, moving = gathered(mine, theirs, moving), None

    step = replicas // 2
    while step:
        upper = bit_of(replica, step)
        there = [at for at, piece in enumerate(pieces) if piece is not None]
        sent = jnp.concatenate([half_of(pieces[at], 1, ~upper) for at in there], 0).astype(jnp.bfloat16)
        if step == 1 and left:
            sent, mine = lax.optimization_barrier((sent, mine))
            moving = left.pop(0)
            row_theirs = swap(mine, "grp", moving)
        theirs = jnp.split(crossed(sent, (0, 0), step).astype(jnp.float32), len(there), axis=0)
        pieces = [piece if piece is None else half_of(piece, 1, upper) for piece in pieces]
        if step == 1:
            kept = [pieces[at] for at in there]
            kept, early_theirs = lax.optimization_barrier((kept, early_theirs))
            for at, piece in zip(there, kept):
                pieces[at] = piece
        for at, block in zip(there, theirs):
            pieces[at ^ step] = add(pieces[at ^ step], block)
        step //= 2
    early += [block.astype(jnp.float32) for block in early_theirs]
    total = ordered([add(*pair) for pair in zip(pieces, early)])

    theirs = None
    for at, steps in enumerate(sum_steps):
        sent = total.astype(jnp.bfloat16)
        answer = crossed(sent, steps, 0)
        if moving:
            sent, row_theirs = lax.optimization_barrier((sent, row_theirs))
            mine, moving = gathered(mine, row_theirs, moving), None
        if left:
            moving = left.pop(0)
            row_theirs = swap(mine, "grp", moving)
        elif theirs is None:
            mine = arranged(mine)
            theirs = swap(mine, "grp", 1)
            if at < len(sum_steps) - 1:
                answer, mine = lax.optimization_barrier((answer, mine))
        if at == len(sum_steps) - 1:
            scaled = halves(ordered(parts))
            grad_pre = matmul(chosen(odd, scaled), mine, ((0,), (0,)))
            grad_pre += matmul(chosen(~odd, scaled), theirs, ((0,), (0,)))
            grad_input = matmul(grad_pre.astype(jnp.bfloat16), weight, ((1,), (1,)))
            answer, grad_input = lax.optimization_barrier((answer, grad_input.astype(jnp.bfloat16)))
        total = sent.astype(jnp.float32) + answer.astype(jnp.float32)

    total = total.astype(jnp.bfloat16)
    other = swap(total, "grp", 1)
    vertex_total = rows * groups * replicas
    swapped = odd ^ upper_half
    product = matmul(total, jnp.where(swapped, theirs, mine), ((0,), (0,)))
    rest = jnp.where(swapped, mine, theirs)
    other, product, rest = lax.optimization_barrier((other, product, rest))
    return (grad_input, final_product(product, other, rest, 1.0 / vertex_total))


def solution(mesh):
    in_specs = (
        P("grp", None),
        P("grp", None),
        P("rep", "grp"),
        P("rep"),
        P("grp"),
        P(("grp", "rep"), None),
        P(),
    )
    out_specs = (P(("grp", "rep"), None), P("rep", None))
    return jax.shard_map(body, mesh=mesh, in_specs=in_specs, out_specs=out_specs, check_vma=False)
```

```python
import functools

import jax
import jax.numpy as jnp
from jax import lax
from jax.experimental import pallas as pl
from jax.experimental.pallas import tpu as pltpu
from jax.sharding import PartitionSpec as P


def swap(block, axis, step):
    size = lax.axis_size(axis)
    return lax.ppermute(block, axis, [(at, at ^ step) for at in range(size)])


def parity(number):
    count = 0
    while number:
        count ^= number & 1
        number >>= 1
    return count


def crossed(block, group_steps, replica_step):
    groups, replicas = lax.axis_size("grp"), lax.axis_size("rep")
    pairs = []
    for group in range(groups):
        for replica in range(replicas):
            step = group_steps[parity(group) ^ parity(replica)]
            step ^= parity(step) ^ parity(replica_step)
            pairs.append((group * replicas + replica, (group ^ step) * replicas + (replica ^ replica_step)))
    return lax.ppermute(block, ("grp", "rep"), pairs)


def bit_of(index, step):
    return (index & step) != 0


def in_order(upper, mine, theirs, axis):
    return jnp.where(
        upper,
        jnp.concatenate([theirs, mine], axis),
        jnp.concatenate([mine, theirs], axis),
    )


def half_of(block, axis, upper):
    size = block.shape[axis] // 2
    low = lax.slice_in_dim(block, 0, size, axis=axis)
    high = lax.slice_in_dim(block, size, 2 * size, axis=axis)
    return jnp.where(upper, high, low)


def part_of(block, axis, index, parts):
    step = parts // 2
    while step:
        block = half_of(block, axis, bit_of(index, step))
        step //= 2
    return block


def add(first, second):
    return second if first is None else first if second is None else first + second


def matmul(left, right, contract):
    return lax.dot_general(
        left, right, (contract, ((), ())), preferred_element_type=jnp.float32
    )


CHUNKS = 4


def prepare_kernel(counts, src_degree, dst_degree, adjoint, active, *refs):
    outs, (src_scale, dst_scale, masked), scratch = refs[:-9], refs[-9:-6], refs[-6:]
    count_part, src_part, dst_part, adjoint_part, active_part, sems = scratch
    src_rows, rows = outs[0].shape
    piece = src_rows // CHUNKS
    replicas = len(outs) + 1
    replica = lax.axis_index("rep")
    owners = [replica ^ step for step in range(1, replicas)]
    degrees = [
        pltpu.make_async_copy(src_degree, src_part, sems.at[0]),
        pltpu.make_async_copy(dst_degree, dst_part, sems.at[1]),
    ]
    factors = [
        pltpu.make_async_copy(adjoint, adjoint_part, sems.at[2]),
        pltpu.make_async_copy(active, active_part, sems.at[3]),
    ]
    copies = []
    for slot, owner in enumerate(owners):
        columns = pl.ds(pl.multiple_of(owner * rows, 128), rows)
        for chunk in range(CHUNKS):
            at = pl.ds(chunk * piece, piece)
            copies.append(
                pltpu.make_async_copy(
                    counts.at[at, columns],
                    count_part.at[slot, at],
                    sems.at[4 + slot * CHUNKS + chunk],
                )
            )
    for copy in degrees + copies + factors:
        copy.start()
    for copy in degrees:
        copy.wait()
    src_row = lax.rsqrt(src_part[...].astype(jnp.float32)).reshape(1, src_rows)
    square = (src_rows, src_rows)
    diagonal = lax.broadcasted_iota(jnp.int32, square, 0) == lax.broadcasted_iota(jnp.int32, square, 1)
    src_column = jnp.sum(
        jnp.where(diagonal, jnp.broadcast_to(src_row, square), 0.0), axis=1, keepdims=True
    )
    src_scale[...] = src_row
    for slot, owner in enumerate(owners + [replica]):
        pieces = [dst_part[at * rows : (at + 1) * rows] for at in range(replicas)]
        bit = 1
        while len(pieces) > 1:
            upper = bit_of(owner, bit)
            pieces = [jnp.where(upper, b, a) for a, b in zip(pieces[0::2], pieces[1::2])]
            bit *= 2
        dst_row = lax.rsqrt(pieces[0].astype(jnp.float32)).reshape(1, rows)
        if slot == len(outs):
            dst_scale[...] = dst_row
            break
        for chunk in range(CHUNKS):
            at = slice(chunk * piece, (chunk + 1) * piece)
            copies[slot * CHUNKS + chunk].wait()
            values = count_part[slot, at, :].astype(jnp.float32)
            outs[slot][at, :] = (values * src_column[at] * dst_row).astype(jnp.bfloat16)
    for copy in factors:
        copy.wait()
    values = adjoint_part[...].astype(jnp.float32) * active_part[...].astype(jnp.float32)
    masked[...] = values.astype(jnp.bfloat16)


def prepare(counts, src_degree, dst_degree, adjoint, active, replicas, rows):
    src_rows, others = counts.shape[0], replicas - 1
    return pl.pallas_call(
        prepare_kernel,
        out_shape=[pltpu.VMEM((src_rows, rows), jnp.bfloat16)] * others
        + [
            pltpu.VMEM((1, src_rows), jnp.float32),
            pltpu.VMEM((1, rows), jnp.float32),
            pltpu.VMEM(adjoint.shape, jnp.bfloat16),
        ],
        in_specs=[pl.BlockSpec(memory_space=pl.ANY)] * 5,
        out_specs=[pl.BlockSpec(memory_space=pltpu.VMEM)] * (others + 3),
        scratch_shapes=[
            pltpu.VMEM((others, src_rows, rows), jnp.int32),
            pltpu.VMEM(src_degree.shape, jnp.int32),
            pltpu.VMEM(dst_degree.shape, jnp.int32),
            pltpu.VMEM(adjoint.shape, adjoint.dtype),
            pltpu.VMEM(active.shape, active.dtype),
            pltpu.SemaphoreType.DMA((4 + CHUNKS * others,)),
        ],
    )(counts, src_degree, dst_degree, adjoint, active)


def own_kernel(own, inputs, term):
    term[...] = jnp.dot(own[...], inputs[...], preferred_element_type=jnp.float32)


def own_product(own, inputs):
    (src_rows, rows), width = own.shape, inputs.shape[1]
    return pl.pallas_call(
        own_kernel,
        out_shape=pltpu.VMEM((src_rows, width), jnp.float32),
        in_specs=[pl.BlockSpec(memory_space=pltpu.VMEM)] * 2,
        out_specs=pl.BlockSpec(memory_space=pltpu.VMEM),
        cost_estimate=pl.CostEstimate(
            flops=2 * src_rows * rows * width,
            bytes_accessed=2 * rows * (src_rows + width),
            transcendentals=0,
        ),
    )(*[pltpu.with_memory_space_constraint(block, pltpu.VMEM) for block in (own, inputs)])


def final_kernel(scale, mine, other, rows, out, parts, sems):
    count, cols, _ = parts.shape
    copies = []
    for at in range(count):
        piece = slice(at * cols, (at + 1) * cols)
        product = matmul(other[:, piece], rows[...], ((0,), (0,)))
        parts[at] = (mine[piece, :] + product) * scale
        copies.append(pltpu.make_async_copy(parts.at[at], out.at[piece, :], sems.at[at]))
        copies[at].start()
    for copy in copies:
        copy.wait()


def final_product(mine, other, rows, scale):
    cols = min(other.shape[1], 128)
    count = other.shape[1] // cols
    return pl.pallas_call(
        functools.partial(final_kernel, scale),
        out_shape=jax.ShapeDtypeStruct(mine.shape, jnp.float32),
        in_specs=[pl.BlockSpec(memory_space=pltpu.VMEM)] * 3,
        out_specs=pl.BlockSpec(memory_space=pl.ANY),
        scratch_shapes=[
            pltpu.VMEM((count, cols, mine.shape[1]), jnp.float32),
            pltpu.SemaphoreType.DMA((count,)),
        ],
    )(*[pltpu.with_memory_space_constraint(block, pltpu.VMEM) for block in (mine, other, rows)])


def body(adjoint, active, counts, src_degree, dst_degree, inputs, weight):
    groups, replicas = lax.axis_size("grp"), lax.axis_size("rep")
    group, replica = lax.axis_index("grp"), lax.axis_index("rep")
    rows, width = inputs.shape
    block_rows = adjoint.shape[0]
    odd = bit_of(group, 1)
    fold = group ^ replica
    shift = 1 << groups.bit_length().bit_length()
    while shift:
        fold ^= fold >> shift
        shift //= 2
    upper_half = bit_of(fold, 1)

    *sent, src_scale, dst_scale, masked = prepare(
        counts, src_degree, dst_degree, adjoint, active, replicas, rows
    )
    answers = [swap(part, "rep", step) for step, part in enumerate(sent, 1)]

    own = part_of(counts, 1, replica, replicas).astype(jnp.float32)
    own = (own * src_scale.reshape(-1, 1) * dst_scale).astype(jnp.bfloat16)
    own_term = own_product(own, inputs)

    far = groups // 2
    others = [far >> at for at in range(1, far.bit_length() - 1)]
    far_steps = [far] * (far > 1)
    sum_steps = list(zip(others + far_steps, others[1:] + far_steps + others[:1]))
    row_steps = far_steps + others

    def gathered(mine, theirs, step):
        upper = bit_of(group, step)
        return in_order(upper, mine[:, None], theirs[:, None], 1).reshape(-1, block_rows, width)

    def arranged(mine):
        split = mine.reshape([2] * len(row_steps) + [block_rows, width])
        order = [row_steps.index(step) for step in far_steps + others]
        return split.transpose(order + [len(order), len(order) + 1]).reshape(-1, width)

    mine = masked.reshape(1, block_rows, width)
    left = list(row_steps)
    moving = None
    if left:
        moving = left.pop(0)
        theirs = swap(mine, "grp", moving)
    parts = [own] + answers

    def ordered(pieces):
        step = 1
        while len(pieces) > 1:
            upper = bit_of(replica, step)
            pieces = [in_order(upper, a, b, 0) for a, b in zip(pieces[0::2], pieces[1::2])]
            step *= 2
        return pieces[0]

    def halves(block):
        pairs = block.reshape(-1, 2, block_rows, block.shape[1])
        even = pairs[:, 0].reshape(-1, block.shape[1])
        uneven = pairs[:, 1].reshape(-1, block.shape[1])
        return even, uneven

    def chosen(upper, pair):
        return jnp.where(upper, pair[1], pair[0])

    def neighbour_sum(block):
        pair = halves(block)
        kept, sent = chosen(upper_half, pair), chosen(~upper_half, pair)
        return kept + swap(sent.astype(jnp.bfloat16), "grp", 1).astype(jnp.float32)

    own_sum = neighbour_sum(own_term)
    early = [part_of(own_sum, 1, replica, replicas)]
    leaving = [
        part_of(own_sum, 1, replica ^ step, replicas).astype(jnp.bfloat16)
        for step in range(1, replicas)
    ]
    answers, early = lax.optimization_barrier((answers, early))
    early_theirs = [crossed(block, (0, 0), step) for step, block in enumerate(leaving, 1)]

    terms = neighbour_sum(jnp.concatenate([matmul(part, inputs, ((1,), (0,))) for part in answers], 0))
    pieces = [None] + jnp.split(terms, replicas - 1, axis=0)
    if moving:
        pieces, theirs = lax.optimization_barrier((pieces, theirs))
        mine, moving = gathered(mine, theirs, moving), None

    step = replicas // 2
    while step:
        upper = bit_of(replica, step)
        there = [at for at, piece in enumerate(pieces) if piece is not None]
        sent = jnp.concatenate([half_of(pieces[at], 1, ~upper) for at in there], 0).astype(jnp.bfloat16)
        if step == 1 and left:
            sent, mine = lax.optimization_barrier((sent, mine))
            moving = left.pop(0)
            row_theirs = swap(mine, "grp", moving)
        theirs = jnp.split(crossed(sent, (0, 0), step).astype(jnp.float32), len(there), axis=0)
        pieces = [piece if piece is None else half_of(piece, 1, upper) for piece in pieces]
        if step == 1:
            kept = [pieces[at] for at in there]
            kept, early_theirs = lax.optimization_barrier((kept, early_theirs))
            for at, piece in zip(there, kept):
                pieces[at] = piece
        for at, block in zip(there, theirs):
            pieces[at ^ step] = add(pieces[at ^ step], block)
        step //= 2
    early += [block.astype(jnp.float32) for block in early_theirs]
    total = ordered([add(*pair) for pair in zip(pieces, early)])

    theirs = None
    for at, steps in enumerate(sum_steps):
        sent = total.astype(jnp.bfloat16)
        answer = crossed(sent, steps, 0)
        if moving:
            sent, row_theirs = lax.optimization_barrier((sent, row_theirs))
            mine, moving = gathered(mine, row_theirs, moving), None
        if left:
            moving = left.pop(0)
            row_theirs = swap(mine, "grp", moving)
        elif theirs is None:
            mine = arranged(mine)
            theirs = swap(mine, "grp", 1)
            if at < len(sum_steps) - 1:
                answer, mine = lax.optimization_barrier((answer, mine))
        if at == len(sum_steps) - 1:
            scaled = halves(ordered(parts))
            grad_pre = matmul(chosen(odd, scaled), mine, ((0,), (0,)))
            grad_pre += matmul(chosen(~odd, scaled), theirs, ((0,), (0,)))
            grad_input = matmul(grad_pre.astype(jnp.bfloat16), weight, ((1,), (1,)))
            answer, grad_input = lax.optimization_barrier((answer, grad_input.astype(jnp.bfloat16)))
        total = sent.astype(jnp.float32) + answer.astype(jnp.float32)

    total = total.astype(jnp.bfloat16)
    other = swap(total, "grp", 1)
    vertex_total = rows * groups * replicas
    swapped = odd ^ upper_half
    product = matmul(total, jnp.where(swapped, theirs, mine), ((0,), (0,)))
    rest = jnp.where(swapped, mine, theirs)
    other, product, rest = lax.optimization_barrier((other, product, rest))
    return (grad_input, final_product(product, other, rest, 1.0 / vertex_total))


def solution(mesh):
    in_specs = (
        P("grp", None),
        P("grp", None),
        P("rep", "grp"),
        P("rep"),
        P("grp"),
        P(("grp", "rep"), None),
        P(),
    )
    out_specs = (P(("grp", "rep"), None), P("rep", None))
    return jax.shard_map(body, mesh=mesh, in_specs=in_specs, out_specs=out_specs, check_vma=False)
```
